32 devices in a mesh: groups: 2 (over x), sect: 8 (over z, y), head: 2 (over core).
Axes of the slice: x: 2, y: 2, z: 4, core: 2. Of those that a mesh axis runs over, the one named last changes fastest.
Arguments:
- queries: bfloat16 [2048, 8192], P(('groups', 'sect'), 'head'), parts along dimension 0, may hold values from -200 to 200
- packed_key_rows: bfloat16 [2048, 512], P(('groups', 'sect'), 'head'), parts along dimension 0, may hold values from -7 to 7
- values: bfloat16 [2048, 512], P(('groups', 'sect'), 'head'), parts along dimension 0, may hold values from -12 to 12
- segments: int32 [2048], P('groups'), parts along dimension 0, may hold values from 0 to 7, never falling along the last dimension, each value on 1 to 512 neighbouring positions
- proj_weight: bfloat16 [8192, 2048], P('head', 'sect'), may hold values from -0.0625 to 0.0625
- residual: bfloat16 [2048, 2048], P(('groups', 'sect', 'head')), parts along dimension 0, may hold values from -2 to 2
- norm_gain: bfloat16 [2048], replicated, may hold values from 0.5 to 1.5
- expert_ids: int32 [2048, 8], P(('groups', 'sect', 'head')), parts along dimension 0, may hold values from 0 to 15, all different within a row; in each aligned block of 64 rows (0 to 63, 64 to 127, ...) at most 48 rows name the same one
- route_weights: float32 [2048, 8], P(('groups', 'sect', 'head')), parts along dimension 0, may hold values from 0.05 to 1
- gate_weight: bfloat16 [16, 2048, 768], P(('sect', 'head')), may hold values from -0.125 to 0.125
- up_weight: bfloat16 [16, 2048, 768], P(('sect', 'head')), may hold values from -0.125 to 0.125
- down_weight: bfloat16 [16, 768, 2048], P(('sect', 'head')), may hold values from -0.21875 to 0.21875
Outputs:
- hidden_mid: bfloat16 [2048, 2048], P(('groups', 'sect', 'head')), parts along dimension 0
- expert_mix: bfloat16 [2048, 2048], P(('groups', 'sect', 'head')), parts along dimension 0
The draws below stay inside these ranges and needn't reach their ends.
There are 2 independent parts, one for each index of `groups`. The reference program is written for one: setup_inputs(seed, part) draws one part's arguments, and reference() takes and returns one part's arrays. A program takes and returns all parts, laid end to end along the dimension named above; an argument that names none is the same for every part. Nothing has to cross between parts.
Inputs may be any that keep to these rules, and one draw needn't show every extreme that they name: `segments`: ids never fall along the rows; each of the 8 prompts has 1 to 512 rows, and one has exactly that many. `expert_ids`: each row names 8 different experts. Within the rows of one device (aligned blocks of 64 rows) no expert is named by more than 48 rows.
All inputs are finite; a program needn't handle non-finite values.
Results may differ from the reference program's by a relative error of at most 0.02.
Values may be sent and summed in bfloat16 or wider, within the bound.
No kernel may reach another device: no remote copies, remote signals or barrier semaphores. Data moves between devices by JAX's collectives and lax.ppermute only.
A program may use at most 256 MiB of HBM per device.

```python
import math
import jax
import jax.numpy as jnp
import numpy as np
from jax import lax

D = 2048
FF = 768
QUERY_HEADS = 64
KEY_VALUE_HEADS = 4
HEAD_WIDTH = 128
TOPK = 8
PROMPTS = 8
SECTION_ROWS = 128
TOKEN_TOTAL = 1024
MOE_ROWS = 64
EXPERTS = 16
CAP = 48
N_SECT = 8
N_HEAD = 2


def base_keys(key):
    unshaped_draw = jax.random.normal(jax.random.fold_in(key, 11), (TOKEN_TOTAL, KEY_VALUE_HEADS, HEAD_WIDTH), jnp.float32)
    return jnp.clip(unshaped_draw, -6.0, 6.0)


def draw_packed_key_rows(key, part):
    key_random_draw = base_keys(key)
    return key_random_draw.reshape(TOKEN_TOTAL, KEY_VALUE_HEADS * HEAD_WIDTH).astype(jnp.bfloat16)


def draw_queries(key, part):
    query_draw = jnp.clip(jax.random.normal(jax.random.fold_in(key, 12), (TOKEN_TOTAL, QUERY_HEADS, HEAD_WIDTH), jnp.float32), -6.0, 6.0)
    return query_draw.reshape(TOKEN_TOTAL, QUERY_HEADS * HEAD_WIDTH).astype(jnp.bfloat16)


def steps_of(key, extent, split, low, top_value):
    factor_of = 1.0
    for position, parts in split:
        draws = jax.random.uniform(jax.random.fold_in(jax.random.fold_in(key, 6), position), (parts,), jnp.float32, low / len(split), top_value / len(split))
        factor_of = factor_of * jnp.repeat(jnp.exp(draws), extent[position] // parts).reshape((-1,) + (1,) * (len(extent) - 1 - position))
    return factor_of


def length_profile(number_of, total, most, slope):
    loads = [(1 << 20) // math.isqrt(standing ** slope) + 1 for standing in range(2, number_of + 1)]
    rest, given = total - most - (number_of - 1), [1] * (number_of - 1)
    while rest > 0:
        movable = [i for i in range(number_of - 1) if given[i] < most]
        whole, budget = sum([loads[i] for i in movable]), rest
        for i in movable:
            addition = min(most - given[i], max(1, budget * loads[i] // whole), rest)
            given[i] = given[i] + addition
            rest = rest - addition
    return np.array([most] + given)


def ragged_sizes(own_key, count, total, most, slope):
    if count == 2:
        one = jax.random.randint(own_key, (), max(1, total - most), min(most, total - 1) + 1)
        return jnp.stack([one, total - one])
    sizes = jnp.asarray(length_profile(count, total, most, slope), jnp.int32)
    pairs = (count - 1) // 2
    giver, receiver = sizes[1:1 + 2 * pairs:2], sizes[2:2 + 2 * pairs:2]
    slack = jnp.minimum(giver - 1, most - receiver)
    shifted = jax.random.randint(jax.random.fold_in(own_key, 1), (pairs,), 0, 1 << 20) % (slack + 1)
    sizes = sizes.at[1:1 + 2 * pairs:2].set(giver - shifted).at[2:2 + 2 * pairs:2].set(receiver + shifted)
    return sizes[jax.random.permutation(jax.random.fold_in(own_key, 2), count)]


def deal_out(key, own, number, rows, count, top, most, skew):
    order = jax.random.permutation(key, count)
    heavy_load, usual = portions_of(count, rows * top, most, skew, True), portions_of(count, rows * top, most, skew, False)
    places = jnp.arange(count)

    def named(sizes, turn):
        used = int((sizes > 0).sum())
        fixed = max(1, used // 4)
        moved = fixed + (places - fixed + turn * (used - fixed)) % max(1, count - fixed)
        return jnp.zeros((count,), jnp.int32).at[order[jnp.where(places < fixed, places, moved)]].set(jnp.asarray(sizes, jnp.int32))

    sizes = jnp.where(number % 4 == 0, named(heavy_load, number // 4), named(usual, number - number // 4 - 1))
    mixed = jax.random.permutation(jax.random.fold_in(own, 3), count)
    donor, receiver = mixed[0:count // 2 * 2:2], mixed[1:count // 2 * 2:2]
    slack = jnp.minimum(sizes[donor] - 1, most - sizes[receiver]) // 2
    slack = jnp.where((donor == order[0]) | (receiver == order[0]) | (sizes[receiver] == 0), 0, jnp.maximum(slack, 0))
    moved = jax.random.randint(jax.random.fold_in(own, 4), (count // 2,), 0, 1 << 20) % (slack + 1)
    sizes = sizes.at[donor].add(-moved).at[receiver].add(moved)
    items = jnp.searchsorted(jnp.cumsum(sizes), jnp.arange(rows * top), side="right").astype(jnp.int32)
    table = items.reshape(top, rows).T
    table = table[jax.random.permutation(jax.random.fold_in(own, 1), rows)]
    turn = jax.random.randint(jax.random.fold_in(own, 2), (rows, 1), 0, top)
    return jnp.take_along_axis(table, (jnp.arange(top)[None, :] + turn) % top, axis=1)


def portions_of(number_of, total, bound, skew, full):
    weights = [(1 << 20) // math.isqrt(rank ** skew) + 1 for rank in range(1, number_of + 1)]
    largest = bound if full else min(bound, max(-(-total // number_of), total * weights[0] // sum(weights)))
    least = 1 if total - largest >= number_of - 1 else 0
    counts, surplus = [largest] + [least] * (number_of - 1), total - largest - least * (number_of - 1)
    while surplus > 0:
        candidates = [i for i in range(1, number_of) if counts[i] < largest] or [i for i in range(1, number_of) if counts[i] < bound]
        mass, remaining = sum([weights[i] for i in candidates]), surplus
        for i in candidates:
            extra = min(bound - counts[i], max(1, remaining * weights[i] // mass), surplus)
            counts[i] = counts[i] + extra
            surplus = surplus - extra
    return np.array(counts)


def scatter_about(key, shape, width, reach, split=(), kind=jnp.bfloat16):
    entries = width * jax.random.normal(key, shape, jnp.float32)
    if split:
        entries = entries * steps_of(key, shape, split, -0.22, 0.18)
    return jnp.clip(entries, -reach, reach).astype(kind)


def setup_inputs(seed: int = 0, part: int = 0) -> dict:
    keys = jax.random.split(jax.random.key(seed), 13)
    part_splits = jax.random.split(jax.random.fold_in(keys[12], part), 13)
    queries = draw_queries(jax.random.fold_in(jax.random.fold_in(keys[12], part), 71), part)
    packed_key_rows = draw_packed_key_rows(jax.random.fold_in(jax.random.fold_in(keys[12], part), 71), part)
    values = scatter_about(part_splits[2], (TOKEN_TOTAL, KEY_VALUE_HEADS * HEAD_WIDTH), 2.0, 12.0, ((0, 8), (1, 2)))
    segments = jnp.searchsorted(jnp.cumsum(ragged_sizes(part_splits[3], PROMPTS, TOKEN_TOTAL, TOKEN_TOTAL // 2, 2)), jnp.arange(TOKEN_TOTAL), side="right").astype(jnp.int32)
    proj_weight = scatter_about(keys[4], (QUERY_HEADS * HEAD_WIDTH, D), (QUERY_HEADS * HEAD_WIDTH) ** -0.5, 0.0625, ((0, 2), (1, 8)))
    residual = scatter_about(part_splits[5], (TOKEN_TOTAL, D), 0.25, 2.0, ((0, 16),))
    norm_gain = jnp.clip(1.0 + 0.1 * jax.random.normal(keys[6], (D,), jnp.float32), 0.5, 1.5).astype(jnp.bfloat16)
    expert_ids_keys = jax.random.split(jax.random.fold_in(part_splits[7], 1), TOKEN_TOTAL // MOE_ROWS)
    expert_ids_turns = jax.random.permutation(jax.random.fold_in(part_splits[7], 3), TOKEN_TOTAL // MOE_ROWS)
    expert_ids = jax.vmap(lambda own, number: deal_out(jax.random.fold_in(part_splits[7], 2), own, number, MOE_ROWS, EXPERTS, TOPK, CAP, 2))(expert_ids_keys, expert_ids_turns).reshape((TOKEN_TOTAL, TOPK))
    route_weights = jnp.clip(jnp.exp(math.log(1.0) - 2.9957323 * jax.random.uniform(part_splits[8], (TOKEN_TOTAL, TOPK), jnp.float32) ** steps_of(part_splits[8], (TOKEN_TOTAL, TOPK), ((0, 16),), -0.2, 0.2)), 0.05, 1.0)
    gate_weight = scatter_about(keys[9], (EXPERTS, D, FF), D ** -0.5, 0.125, ((0, 16),))
    up_weight = scatter_about(keys[10], (EXPERTS, D, FF), D ** -0.5, 0.125, ((0, 16),))
    down_weight = scatter_about(keys[11], (EXPERTS, FF, D), FF ** -0.5, 0.21875, ((0, 16),))
    return {"queries": queries, "packed_key_rows": packed_key_rows, "values": values, "segments": segments, "proj_weight": proj_weight, "residual": residual, "norm_gain": norm_gain, "expert_ids": expert_ids, "route_weights": route_weights, "gate_weight": gate_weight, "up_weight": up_weight, "down_weight": down_weight}


negative_large = -1e+30
norm_eps = 1e-06

def attention_block(block_pos, queries, packed_key_rows, values, segments):
    query_group_width = QUERY_HEADS // KEY_VALUE_HEADS
    key_window_length = min(128, TOKEN_TOTAL)
    key_block_count = TOKEN_TOTAL // key_window_length
    beginning_row = (block_pos * SECTION_ROWS).astype(jnp.int32)
    query_tensor_four = lax.dynamic_slice_in_dim(queries, beginning_row, SECTION_ROWS, 0).astype(jnp.float32).reshape(SECTION_ROWS, KEY_VALUE_HEADS, query_group_width, HEAD_WIDTH)
    query_pos = beginning_row + jnp.arange(SECTION_ROWS, dtype=jnp.int32)
    query_seg = lax.dynamic_slice_in_dim(segments, beginning_row, SECTION_ROWS, 0)
    seg_start = lax.optimization_barrier(jnp.sum((segments[None, :] < query_seg[:, None]).astype(jnp.int32), axis=1))
    lowest = jnp.min(seg_start)
    highest = jnp.max(query_pos)
    score_scale = 1.0 / math.sqrt(HEAD_WIDTH)

    def piece_scores(block_index):
        key_begin_index = (block_index * key_window_length).astype(jnp.int32)
        key_tensor_three = lax.dynamic_slice_in_dim(packed_key_rows, key_begin_index, key_window_length, 0).astype(jnp.float32).reshape(key_window_length, KEY_VALUE_HEADS, HEAD_WIDTH)
        scores = jnp.einsum('rkgd,pkd->rkgp', query_tensor_four, key_tensor_three, precision=lax.Precision.HIGHEST) * score_scale
        key_pos = key_begin_index + jnp.arange(key_window_length, dtype=jnp.int32)
        key_seg = lax.dynamic_slice_in_dim(segments, key_begin_index, key_window_length, 0)
        allowed = jnp.logical_and(key_seg[None, :] == query_seg[:, None], key_pos[None, :] <= query_pos[:, None])
        return (scores, allowed[:, None, None, :], key_begin_index)

    def needed(block_index):
        key_begin_index = block_index * key_window_length
        return jnp.logical_and(key_begin_index <= highest, key_begin_index + key_window_length - 1 >= lowest)

    def maximum_update(block_index, run_max):

        def compute(current):
            scores, allowed, key_begin_index = piece_scores(block_index)
            return jnp.maximum(current, lax.optimization_barrier(jnp.max(jnp.where(allowed, scores, negative_large), axis=-1)))
        return lax.cond(needed(block_index), compute, lambda running: running, run_max)
    row_maximum = lax.fori_loop(0, key_block_count, maximum_update, jnp.full((SECTION_ROWS, KEY_VALUE_HEADS, query_group_width), negative_large, jnp.float32))

    def sum_step(block_index, running):

        def compute(current):
            weight_sum, run_acc = current
            scores, allowed, key_begin_index = piece_scores(block_index)
            weights = jnp.where(allowed, jnp.exp(scores - row_maximum[..., None]), 0.0).astype(jnp.bfloat16)
            weights = lax.optimization_barrier(weights).astype(jnp.float32)
            value_tensor_three = lax.dynamic_slice_in_dim(values, key_begin_index, key_window_length, 0).astype(jnp.float32).reshape(key_window_length, KEY_VALUE_HEADS, HEAD_WIDTH)
            run_acc = run_acc + jnp.einsum('rkgp,pkd->rkgd', weights, value_tensor_three, precision=lax.Precision.HIGHEST)
            return (weight_sum + lax.optimization_barrier(jnp.sum(weights, axis=-1)), run_acc)
        return lax.cond(needed(block_index), compute, lambda kept: kept, running)
    initial_state = (jnp.zeros((SECTION_ROWS, KEY_VALUE_HEADS, query_group_width), jnp.float32), jnp.zeros((SECTION_ROWS, KEY_VALUE_HEADS, query_group_width, HEAD_WIDTH), jnp.float32))
    weight_sum, run_acc = lax.fori_loop(0, key_block_count, sum_step, initial_state)
    return (run_acc / weight_sum[..., None]).reshape(SECTION_ROWS, QUERY_HEADS * HEAD_WIDTH).astype(jnp.bfloat16)

def reference(queries, packed_key_rows, values, segments, proj_weight, residual, norm_gain, expert_ids, route_weights, gate_weight, up_weight, down_weight):
    attended = lax.map(lambda block_pos: attention_block(block_pos, queries, packed_key_rows, values, segments), jnp.arange(TOKEN_TOTAL // SECTION_ROWS, dtype=jnp.int32))
    attended = attended.reshape(TOKEN_TOTAL, QUERY_HEADS * HEAD_WIDTH)
    projected = jnp.dot(attended, proj_weight, preferred_element_type=jnp.float32)
    hidden_mid = (residual.astype(jnp.float32) + projected).astype(jnp.bfloat16)
    mid_float = lax.optimization_barrier(hidden_mid).astype(jnp.float32)
    inverse = lax.rsqrt(lax.optimization_barrier(jnp.mean(mid_float * mid_float, axis=1, keepdims=True)) + norm_eps)
    normed = (mid_float * inverse * norm_gain.astype(jnp.float32)[None, :]).astype(jnp.bfloat16)
    route_share = (route_weights / lax.optimization_barrier(jnp.sum(route_weights, axis=1, keepdims=True))).reshape(-1)
    flat_ids = expert_ids.reshape(-1)
    slot_total = N_SECT * N_HEAD * CAP

    def expert_step(mixture, expert):
        named = flat_ids == expert
        picked = jnp.nonzero(named, size=slot_total, fill_value=0)[0].astype(jnp.int32)
        valid_slot = jnp.arange(slot_total, dtype=jnp.int32) < jnp.sum(named.astype(jnp.int32))
        row_ids = picked // TOPK
        inputs = normed[row_ids]
        gate_act = jnp.dot(inputs, gate_weight[expert], preferred_element_type=jnp.float32)
        up_act = jnp.dot(inputs, up_weight[expert], preferred_element_type=jnp.float32)
        hidden = (jax.nn.silu(gate_act) * up_act).astype(jnp.bfloat16)
        result = jnp.dot(hidden, down_weight[expert], preferred_element_type=jnp.float32).astype(jnp.bfloat16)
        result = lax.optimization_barrier(result).astype(jnp.float32)
        weight = jnp.where(valid_slot, route_share[picked], 0.0)
        mixture = mixture.at[row_ids].add(weight[:, None] * result)
        return (mixture, None)
    mixture, unused = lax.scan(expert_step, jnp.zeros((TOKEN_TOTAL, D), jnp.float32), jnp.arange(EXPERTS, dtype=jnp.int32))
    return (hidden_mid, mixture.astype(jnp.bfloat16))
```

```python
import functools
import math

import jax
import jax.numpy as jnp
from jax import lax
from jax.experimental import pallas as pl
from jax.experimental.pallas import tpu as pltpu
from jax.sharding import PartitionSpec as P

HEAD_WIDTH = 128

negative_large = -1e30
norm_eps = 1e-06


def swap(value, axis, bit):
    count = lax.axis_size(axis)
    return lax.ppermute(value, axis, [(i, i ^ bit) for i in range(count)])


def shift(value, axis, step):
    count = lax.axis_size(axis)
    return lax.ppermute(value, axis, [(i, i + step) for i in range(count - step)])


def attend_kernel(heads, scale, bias_ref, query_ref, *refs):
    *kv_refs, out_ref = refs
    rows = kv_refs[0].shape[0] // 2
    keys = jnp.concatenate([kv[:rows, :] for kv in kv_refs], axis=0)
    vals = jnp.concatenate([kv[rows:, :] for kv in kv_refs], axis=0)
    vals = jnp.concatenate([vals, jnp.ones_like(vals)], axis=1)
    for head in range(heads):
        cols = slice(head * HEAD_WIDTH, (head + 1) * HEAD_WIDTH)
        scores = lax.dot_general(
            query_ref[:, cols], keys, (((1,), (1,)), ((), ())), preferred_element_type=jnp.float32
        )
        scores = scores * scale + bias_ref[...]
        top = jnp.max(scores, axis=1, keepdims=True)
        weights = jnp.exp2(scores - top).astype(jnp.bfloat16)
        mixed = jnp.dot(weights, vals, preferred_element_type=jnp.float32)
        out_ref[:, cols] = (mixed[:, :HEAD_WIDTH] / mixed[:, HEAD_WIDTH:]).astype(jnp.bfloat16)


def attend(queries, kv_blocks, bias, kv_index, kv_heads):
    rows = queries.shape[0]
    width = queries.shape[1] // kv_heads
    heads = width // HEAD_WIDTH
    step_heads = min(4, heads)
    steps = heads // step_heads
    block = step_heads * HEAD_WIDTH
    keys = bias.shape[1]
    scale = math.log2(math.e) / math.sqrt(HEAD_WIDTH)
    return pl.pallas_call(
        functools.partial(attend_kernel, step_heads, scale),
        out_shape=jax.ShapeDtypeStruct((rows, width), jnp.bfloat16),
        grid=(steps,),
        in_specs=[
            pl.BlockSpec((rows, keys), lambda i: (0, 0)),
            pl.BlockSpec((rows, block), lambda i: (0, kv_index * steps + i)),
        ]
        + [pl.BlockSpec((2 * rows, HEAD_WIDTH), lambda i: (0, kv_index)) for _ in kv_blocks],
        out_specs=pl.BlockSpec((rows, block), lambda i: (0, i)),
        compiler_params=pltpu.CompilerParams(vmem_limit_bytes=40 * 1024 * 1024),
        cost_estimate=pl.CostEstimate(
            flops=6 * rows * keys * width,
            bytes_accessed=4 * rows * width + 4 * rows * keys * len(kv_blocks),
            transcendentals=rows * keys * heads,
        ),
        name="attend",
    )(bias, queries, *kv_blocks)


def norm_kernel(blocks_ref, part_ref, residual_ref, gain_ref, hidden_ref, normed_ref):
    offsets, rows, width = part_ref.shape
    half = width // 2
    total = jnp.zeros((rows, 1), jnp.float32)
    for off in range(offsets):
        for upper in range(2):
            col = pl.multiple_of(blocks_ref[off + upper * offsets] * half, half)
            cols = pl.ds(col, half)
            part = part_ref[off, :, upper * half : (upper + 1) * half]
            hidden = (residual_ref[:, cols].astype(jnp.float32) + part).astype(jnp.bfloat16)
            hidden_ref[:, cols] = hidden
            wide = hidden.astype(jnp.float32)
            total = total + jnp.sum(wide * wide, axis=1, keepdims=True)
    inverse = lax.rsqrt(total / (2 * offsets * half) + norm_eps)
    wide = hidden_ref[...].astype(jnp.float32)
    normed_ref[...] = (wide * inverse * gain_ref[...].astype(jnp.float32)).astype(jnp.bfloat16)


def norm_rows(parts, residual, gain, block_index):
    offsets, rows, width = parts.shape
    if (width // 2) % 128:
        blocks = parts.reshape(offsets, rows, 2, width // 2).transpose(2, 0, 1, 3)
        blocks = blocks.reshape(2 * offsets, rows, width // 2)[block_index]
        wide = blocks.transpose(1, 0, 2).reshape(residual.shape).astype(jnp.float32)
        hidden = (residual.astype(jnp.float32) + wide).astype(jnp.bfloat16)
        wide = hidden.astype(jnp.float32)
        inverse = lax.rsqrt(jnp.mean(wide * wide, axis=1, keepdims=True) + norm_eps)
        return hidden, (wide * inverse * gain.astype(jnp.float32)[None, :]).astype(jnp.bfloat16)
    vmem = pl.BlockSpec(memory_space=pltpu.VMEM)
    return pl.pallas_call(
        norm_kernel,
        out_shape=(
            jax.ShapeDtypeStruct(residual.shape, jnp.bfloat16),
            jax.ShapeDtypeStruct(residual.shape, jnp.bfloat16),
        ),
        in_specs=[pl.BlockSpec(memory_space=pltpu.SMEM), vmem, vmem, vmem],
        out_specs=(vmem, vmem),
        name="norm_rows",
    )(block_index, parts, residual, gain.reshape(1, -1))


def shards(
    queries,
    packed_key_rows,
    values,
    segments,
    proj_weight,
    residual,
    norm_gain,
    expert_ids,
    route_weights,
    gate_weight,
    up_weight,
    down_weight,
):
    rows = queries.shape[0]
    total_rows = segments.shape[0]
    sect_count = lax.axis_size("sect")
    head_count = lax.axis_size("head")
    group_count = lax.axis_size("groups")
    sect_pos = lax.axis_index("sect")
    head_pos = lax.axis_index("head")
    group_pos = lax.axis_index("groups")
    kv_heads = packed_key_rows.shape[1] // HEAD_WIDTH
    experts = sect_count * head_count
    moe_rows = residual.shape[0]
    top_bit = sect_count // 2

    back = min(sect_count - 1, -(-(total_rows // 2 - 1) // rows))
    own_kv = jnp.concatenate([packed_key_rows, values], axis=0)
    kv_blocks = [shift(own_kv, "sect", step) for step in range(back, 0, -1)] + [own_kv]

    depth = proj_weight.shape[0]
    part_depth = depth // group_count
    pieces = 4
    piece_depth = part_depth // pieces
    fetched = [[None] * pieces for _ in range(group_count)]
    for piece in range(pieces):
        start = group_pos * part_depth + piece * piece_depth
        mine = lax.dynamic_slice_in_dim(proj_weight, start, piece_depth, 0)
        fetched[0][piece] = swap(mine, "sect", top_bit)
        for other in range(1, group_count):
            fetched[other][piece] = swap(fetched[0][piece], "groups", other)

    route_share = route_weights / jnp.sum(route_weights, axis=1, keepdims=True)
    named = expert_ids[:, :, None] == jnp.arange(experts, dtype=jnp.int32)[None, None, :]
    combine = jnp.sum(jnp.where(named, route_share[:, :, None], 0.0), axis=1)
    combine_all = lax.all_gather(combine, ("sect", "head"), axis=0, tiled=True)

    own_start = sect_pos * rows
    window = (back + 1) * rows
    padded = jnp.pad(segments, (back * rows, 0), constant_values=-1)
    key_seg = lax.dynamic_slice_in_dim(padded, own_start, window, 0)
    query_seg = key_seg[back * rows :]
    key_pos = jnp.arange(window, dtype=jnp.int32)
    query_pos = back * rows + jnp.arange(rows, dtype=jnp.int32)
    allowed = jnp.logical_and(
        key_seg[None, :] == query_seg[:, None], key_pos[None, :] <= query_pos[:, None]
    )
    bias = jnp.where(allowed, 0.0, negative_large).astype(jnp.float32)
    low_bits = []
    bit = 1
    while bit < top_bit:
        low_bits.append(bit)
        bit *= 2
    gathered = []
    for kv_index in range(kv_heads):
        attended = attend(queries, kv_blocks, bias, kv_index, kv_heads)
        held = {0: attended}
        for bit in low_bits if kv_index % 2 else low_bits[::-1]:
            for offset in list(held):
                held[offset ^ bit] = swap(held[offset], "sect", bit)
        gathered.append(jnp.concatenate([held[off] for off in range(top_bit)], axis=0))

    stacked = jnp.stack([jnp.concatenate(fetched[g], axis=0) for g in range(group_count)])
    parts = [
        lax.dynamic_index_in_dim(stacked, group_pos ^ g, 0, keepdims=False)
        for g in range(group_count)
    ]
    far = jnp.concatenate(parts, axis=0)
    rows_all = jnp.concatenate(gathered, axis=1)
    block = jnp.concatenate(
        [
            jnp.dot(rows_all, proj_weight, preferred_element_type=jnp.float32),
            jnp.dot(rows_all, far, preferred_element_type=jnp.float32),
        ],
        axis=1,
    ).reshape(top_bit, head_count, moe_rows, -1)
    kept = lax.dynamic_index_in_dim(block, head_pos, 1, keepdims=False)
    sent = lax.dynamic_index_in_dim(block, 1 - head_pos, 1, keepdims=False)
    summed = kept + swap(sent.astype(jnp.bfloat16), "head", 1).astype(jnp.float32)
    summed = summed.astype(jnp.bfloat16)
    own_parts = [summed[0]] + [swap(summed[off], "sect", off) for off in range(1, top_bit)]
    block_index = sect_pos ^ jnp.arange(sect_count, dtype=jnp.int32)
    hidden_mid, normed = norm_rows(jnp.stack(own_parts), residual, norm_gain, block_index)

    even = list(range(0, sect_count, 2))
    pieces_in = {0: normed}
    for off in even[1:]:
        pieces_in[off] = swap(normed, "sect", off)
    for off in even:
        pieces_in[off ^ 1] = swap(pieces_in[off], "sect", 1)
    flipped = {off: swap(pieces_in[off], "head", 1) for off in range(sect_count)}

    own_expert = sect_pos * head_count + head_pos
    own_combine = lax.dynamic_index_in_dim(combine_all, own_expert, 1, keepdims=False)
    own_combine = own_combine.reshape(experts, moe_rows)
    order = (block_index[:, None] * head_count) + (
        head_pos ^ jnp.arange(head_count, dtype=jnp.int32)[None, :]
    )
    own_combine = own_combine[order.reshape(-1)].reshape(sect_count, head_count * moe_rows)

    def expert_rows(offs):
        flat = jnp.concatenate([p for off in offs for p in (pieces_in[off], flipped[off])], axis=0)
        gate_act = jnp.dot(flat, gate_weight[0], preferred_element_type=jnp.float32)
        up_act = jnp.dot(flat, up_weight[0], preferred_element_type=jnp.float32)
        hidden = (jax.nn.silu(gate_act) * up_act).astype(jnp.bfloat16)
        result = jnp.dot(hidden, down_weight[0], preferred_element_type=jnp.float32)
        share = jnp.concatenate([own_combine[off] for off in offs])[:, None]
        result = result.astype(jnp.bfloat16).astype(jnp.float32) * share
        result = result.reshape(len(offs), head_count, moe_rows, -1)
        return result[:, 0], result[:, 1].astype(jnp.bfloat16)

    final = None
    for off in even:
        kept, sent = expert_rows((off, off ^ 1))
        summed = kept + swap(sent, "head", 1).astype(jnp.float32)
        across = swap(summed[1].astype(jnp.bfloat16), "sect", 1).astype(jnp.float32)
        section = summed[0] + across
        if off:
            section = swap(section.astype(jnp.bfloat16), "sect", off).astype(jnp.float32)
        final = section if final is None else final + section
    return (hidden_mid, final.astype(jnp.bfloat16))


def solution(mesh):
    placed = (
        P(("groups", "sect"), "head"),
        P(("groups", "sect"), "head"),
        P(("groups", "sect"), "head"),
        P("groups"),
        P("head", "sect"),
        P(("groups", "sect", "head"), None),
        P(),
        P(("groups", "sect", "head"), None),
        P(("groups", "sect", "head"), None),
        P(("sect", "head"), None, None),
        P(("sect", "head"), None, None),
        P(("sect", "head"), None, None),
    )
    return jax.shard_map(
        shards,
        mesh=mesh,
        in_specs=placed,
        out_specs=(P(("groups", "sect", "head"), None), P(("groups", "sect", "head"), None)),
        check_vma=False,
    )
```

```python
import functools
import math

import jax
import jax.numpy as jnp
from jax import lax
from jax.experimental import pallas as pl
from jax.experimental.pallas import tpu as pltpu
from jax.sharding import PartitionSpec as P

HEAD_WIDTH = 128

GRANT = 56 * 1024 * 1024

negative_large = -1e30
norm_eps = 1e-06


def swap(value, axis, bit):
    count = lax.axis_size(axis)
    return lax.ppermute(value, axis, [(i, i ^ bit) for i in range(count)])


def after(values, others):
    return lax.optimization_barrier((tuple(values), tuple(others)))[0]


def shift(value, axis, step):
    count = lax.axis_size(axis)
    return lax.ppermute(value, axis, [(i, i + step) for i in range(count - step)])


def attend_kernel(heads, scale, bias_ref, query_ref, *refs):
    *kv_refs, out_ref = refs
    rows = kv_refs[0].shape[0] // 2
    keys = jnp.concatenate([kv[:rows, :] for kv in kv_refs], axis=0)
    vals = jnp.concatenate([kv[rows:, :] for kv in kv_refs], axis=0)
    vals = jnp.concatenate([vals, jnp.ones_like(vals)], axis=1)
    for head in range(heads):
        cols = slice(head * HEAD_WIDTH, (head + 1) * HEAD_WIDTH)
        scores = lax.dot_general(
            query_ref[:, cols], keys, (((1,), (1,)), ((), ())), preferred_element_type=jnp.float32
        )
        scores = scores * scale + bias_ref[...]
        top = jnp.max(scores, axis=1, keepdims=True)
        weights = jnp.exp2(scores - top).astype(jnp.bfloat16)
        mixed = jnp.dot(weights, vals, preferred_element_type=jnp.float32)
        out_ref[:, cols] = (mixed[:, :HEAD_WIDTH] / mixed[:, HEAD_WIDTH:]).astype(jnp.bfloat16)


def attend(queries, kv_blocks, bias, kv_index, kv_heads):
    rows = queries.shape[0]
    width = queries.shape[1] // kv_heads
    heads = width // HEAD_WIDTH
    step_heads = min(4, heads)
    steps = heads // step_heads
    block = step_heads * HEAD_WIDTH
    keys = bias.shape[1]
    scale = math.log2(math.e) / math.sqrt(HEAD_WIDTH)
    return pl.pallas_call(
        functools.partial(attend_kernel, step_heads, scale),
        out_shape=jax.ShapeDtypeStruct((rows, width), jnp.bfloat16),
        grid=(steps,),
        in_specs=[
            pl.BlockSpec((rows, keys), lambda i: (0, 0)),
            pl.BlockSpec((rows, block), lambda i: (0, kv_index * steps + i)),
        ]
        + [pl.BlockSpec((2 * rows, HEAD_WIDTH), lambda i: (0, kv_index)) for _ in kv_blocks],
        out_specs=pl.BlockSpec((rows, block), lambda i: (0, i)),
        compiler_params=pltpu.CompilerParams(vmem_limit_bytes=GRANT),
        cost_estimate=pl.CostEstimate(
            flops=6 * rows * keys * width,
            bytes_accessed=4 * rows * width + 4 * rows * keys * len(kv_blocks),
            transcendentals=rows * keys * heads,
        ),
        name="attend",
    )(bias, queries, *kv_blocks)


def norm_kernel(
    experts, blocks_ref, part_ref, residual_ref, gain_ref, combine_ref, hidden_ref, normed_ref
):
    offsets, rows, width = part_ref.shape
    half = width // 2
    columns = 2 * offsets * half
    total = jnp.zeros((rows, 1), jnp.float32)
    for off in range(offsets):
        for upper in range(2):
            col = pl.multiple_of(blocks_ref[off + upper * offsets] * half, half)
            cols = pl.ds(col, half)
            part = part_ref[off, :, upper * half : (upper + 1) * half]
            hidden = (residual_ref[:, cols].astype(jnp.float32) + part).astype(jnp.bfloat16)
            hidden_ref[:, cols] = hidden
            wide = hidden.astype(jnp.float32)
            total = total + jnp.sum(wide * wide, axis=1, keepdims=True)
    inverse = lax.rsqrt(total / columns + norm_eps)
    wide = hidden_ref[...].astype(jnp.float32)
    wide = wide * inverse * gain_ref[...].astype(jnp.float32)
    normed_ref[:, :columns] = wide.astype(jnp.bfloat16)
    normed_ref[:, columns:] = split_combine(combine_ref[...], experts)


def split_combine(combine, experts):
    high = combine.astype(jnp.bfloat16).astype(jnp.float32)
    lane = lax.broadcasted_iota(jnp.int32, combine.shape, 1)
    return jnp.where(lane < experts, high, combine - high).astype(jnp.bfloat16)


def norm_rows(parts, residual, gain, combine, experts, block_index):
    offsets, rows, width = parts.shape
    if (width // 2) % 128:
        blocks = parts.reshape(offsets, rows, 2, width // 2).transpose(2, 0, 1, 3)
        blocks = blocks.reshape(2 * offsets, rows, width // 2)[block_index]
        wide = blocks.transpose(1, 0, 2).reshape(residual.shape).astype(jnp.float32)
        hidden = (residual.astype(jnp.float32) + wide).astype(jnp.bfloat16)
        wide = hidden.astype(jnp.float32)
        inverse = lax.rsqrt(jnp.mean(wide * wide, axis=1, keepdims=True) + norm_eps)
        normed = (wide * inverse * gain.astype(jnp.float32)[None, :]).astype(jnp.bfloat16)
        high = lax.reduce_precision(combine, 8, 7)
        lane = lax.broadcasted_iota(jnp.int32, combine.shape, 1)
        split = jnp.where(lane < experts, high, combine - high).astype(jnp.bfloat16)
        return hidden, jnp.concatenate([normed, split], axis=1)
    vmem = pl.BlockSpec(memory_space=pltpu.VMEM)
    return pl.pallas_call(
        functools.partial(norm_kernel, experts),
        out_shape=(
            jax.ShapeDtypeStruct(residual.shape, jnp.bfloat16),
            jax.ShapeDtypeStruct((rows, residual.shape[1] + combine.shape[1]), jnp.bfloat16),
        ),
        in_specs=[pl.BlockSpec(memory_space=pltpu.SMEM), vmem, vmem, vmem, vmem],
        out_specs=(vmem, vmem),
        name="norm_rows",
    )(block_index, parts, residual, gain.reshape(1, -1), combine)


def project_kernel(kv_heads, offsets, place_ref, *refs):
    count = kv_heads * offsets
    rows_refs = refs[:count]
    own_ref = refs[count]
    *far_refs, kept_ref, sent_ref, all_ref, near_ref, upper_ref, sems = refs[count + 1 :]
    head = place_ref[0]
    rows, width = rows_refs[0].shape
    half = rows // 2
    depth = far_refs[0].shape[0]
    copies = [pltpu.make_async_copy(own_ref, near_ref, sems.at[count])]
    for kv_index in range(kv_heads):
        for off in range(offsets):
            index = kv_index * offsets + off
            target = all_ref.at[
                pl.ds(off * rows, rows), pl.ds(kv_index * width, width)
            ]
            copies.append(pltpu.make_async_copy(rows_refs[index], target, sems.at[index]))
    far_copies = []
    for index, far_ref in enumerate(far_refs):
        target = upper_ref.at[pl.ds(index * depth, depth), :]
        far_copies.append(pltpu.make_async_copy(far_ref, target, sems.at[count + 1 + index]))
    for copy in copies + far_copies:
        copy.start()
    for copy in copies:
        copy.wait()
    near = jnp.dot(all_ref[...], near_ref[...], preferred_element_type=jnp.float32)
    far = None
    for index, copy in enumerate(far_copies):
        copy.wait()
        start = pl.multiple_of(place_ref[1 + index] * depth, depth)
        product = jnp.dot(
            all_ref[:, pl.ds(start, depth)],
            upper_ref[index * depth : (index + 1) * depth, :],
            preferred_element_type=jnp.float32,
        )
        far = product if far is None else far + product
    columns = near.shape[1]
    for off in range(offsets):
        for upper, block in enumerate((near, far)):
            cols = slice(upper * columns, (upper + 1) * columns)
            first = block[off * rows : off * rows + half]
            second = block[off * rows + half : (off + 1) * rows]
            kept_ref[off, :, cols] = jnp.where(head == 0, first, second)
            sent_ref[off, :, cols] = jnp.where(head == 0, second, first).astype(jnp.bfloat16)


def project(pieces, own_weight, far_pieces, place):
    kv_heads, offsets = len(pieces), len(pieces[0])
    rows, width = pieces[0][0].shape
    columns = own_weight.shape[1]
    vmem = pl.BlockSpec(memory_space=pltpu.VMEM)
    flat = [piece for group in pieces for piece in group]
    shape = (offsets, rows // 2, 2 * columns)
    return pl.pallas_call(
        functools.partial(project_kernel, kv_heads, offsets),
        out_shape=(
            jax.ShapeDtypeStruct(shape, jnp.float32),
            jax.ShapeDtypeStruct(shape, jnp.bfloat16),
        ),
        in_specs=[pl.BlockSpec(memory_space=pltpu.SMEM)]
        + [pl.BlockSpec(memory_space=pl.ANY)] * (len(flat) + 1 + len(far_pieces)),
        out_specs=(vmem, vmem),
        scratch_shapes=[
            pltpu.VMEM((offsets * rows, kv_heads * width), jnp.bfloat16),
            pltpu.VMEM(own_weight.shape, jnp.bfloat16),
            pltpu.VMEM(own_weight.shape, jnp.bfloat16),
            pltpu.SemaphoreType.DMA((len(flat) + 1 + len(far_pieces),)),
        ],
        compiler_params=pltpu.CompilerParams(vmem_limit_bytes=GRANT),
        cost_estimate=pl.CostEstimate(
            flops=4 * offsets * rows * kv_heads * width * columns,
            bytes_accessed=4 * kv_heads * width * columns,
            transcendentals=0,
        ),
        name="project",
    )(place, *flat, own_weight, *far_pieces)


def expert_kernel(experts, pieces, place_ref, *refs):
    piece_refs = refs[:pieces]
    gate_ref, up_ref, down_ref, kept_ref, sent_ref = refs[pieces : pieces + 5]
    rows_ref, mid_ref, sems = refs[pieces + 5 :]
    rows = piece_refs[0].shape[0]
    depth, inner = gate_ref.shape[1:]
    copies = [
        pltpu.make_async_copy(ref, rows_ref.at[pl.ds(i * rows, rows), :], sems.at[i])
        for i, ref in enumerate(piece_refs)
    ]
    for copy in copies:
        copy.start()
    for copy in copies:
        copy.wait()
    extra = rows_ref[:, depth:].astype(jnp.float32)
    lane = lax.broadcasted_iota(jnp.int32, extra.shape, 1)
    own = jnp.logical_or(lane == place_ref[0], lane == place_ref[0] + experts)
    share = jnp.sum(jnp.where(own, extra, 0.0), axis=1, keepdims=True)
    tile = math.gcd(inner, 256)
    for start in range(0, inner, tile):
        cols = slice(start, start + tile)
        flat = rows_ref[:, :depth]
        gate = jnp.dot(flat, gate_ref[0, :, cols], preferred_element_type=jnp.float32)
        up = jnp.dot(flat, up_ref[0, :, cols], preferred_element_type=jnp.float32)
        mid_ref[:, cols] = (gate / (1.0 + jnp.exp(-gate)) * up).astype(jnp.bfloat16)
    tile = math.gcd(depth, 512)
    for start in range(0, depth, tile):
        cols = slice(start, start + tile)
        out = jnp.dot(mid_ref[...], down_ref[0, :, cols], preferred_element_type=jnp.float32)
        out = out.astype(jnp.bfloat16).astype(jnp.float32) * share
        for index in range(pieces):
            part = out[index * rows : (index + 1) * rows]
            if index % 2:
                sent_ref[index // 2, :, cols] = part.astype(jnp.bfloat16)
            else:
                kept_ref[index // 2, :, cols] = part


def expert_rows(pieces, gate_weight, up_weight, down_weight, experts, place):
    rows = pieces[0].shape[0]
    depth, inner = gate_weight.shape[1:]
    count = len(pieces)
    vmem = pl.BlockSpec(memory_space=pltpu.VMEM)
    shape = (count // 2, rows, depth)
    return pl.pallas_call(
        functools.partial(expert_kernel, experts, count),
        out_shape=(
            jax.ShapeDtypeStruct(shape, jnp.float32),
            jax.ShapeDtypeStruct(shape, jnp.bfloat16),
        ),
        in_specs=[pl.BlockSpec(memory_space=pltpu.SMEM)]
        + [pl.BlockSpec(memory_space=pl.ANY)] * count
        + [vmem] * 3,
        out_specs=(vmem, vmem),
        scratch_shapes=[
            pltpu.VMEM((count * rows, pieces[0].shape[1]), jnp.bfloat16),
            pltpu.VMEM((count * rows, inner), jnp.bfloat16),
            pltpu.SemaphoreType.DMA((count,)),
        ],
        compiler_params=pltpu.CompilerParams(vmem_limit_bytes=16 * 1024 * 1024),
        cost_estimate=pl.CostEstimate(
            flops=6 * count * rows * depth * inner,
            bytes_accessed=6 * depth * inner,
            transcendentals=count * rows * inner,
        ),
        name="expert_rows",
    )(place, *pieces, gate_weight, up_weight, down_weight)


def shards(
    queries,
    packed_key_rows,
    values,
    segments,
    proj_weight,
    residual,
    norm_gain,
    expert_ids,
    route_weights,
    gate_weight,
    up_weight,
    down_weight,
):
    rows = queries.shape[0]
    total_rows = segments.shape[0]
    sect_count = lax.axis_size("sect")
    head_count = lax.axis_size("head")
    group_count = lax.axis_size("groups")
    sect_pos = lax.axis_index("sect")
    head_pos = lax.axis_index("head")
    group_pos = lax.axis_index("groups")
    kv_heads = packed_key_rows.shape[1] // HEAD_WIDTH
    experts = sect_count * head_count
    moe_rows = residual.shape[0]
    top_bit = sect_count // 2

    back = min(sect_count - 1, -(-(total_rows // 2 - 1) // rows))
    own_kv = jnp.concatenate([packed_key_rows, values], axis=0)
    kv_blocks = [shift(own_kv, "sect", step) for step in range(back, 0, -1)] + [own_kv]

    depth = proj_weight.shape[0]
    part_depth = depth // group_count
    pieces = 2
    piece_depth = part_depth // pieces
    source, *kv_blocks = lax.optimization_barrier((proj_weight, *kv_blocks))
    fetched = [[None] * pieces for _ in range(group_count)]
    for piece in range(pieces):
        start = group_pos * part_depth + piece * piece_depth
        mine = lax.dynamic_slice_in_dim(source, start, piece_depth, 0)
        fetched[0][piece] = swap(mine, "sect", top_bit)
    route_share = route_weights / jnp.sum(route_weights, axis=1, keepdims=True)
    named = expert_ids[:, :, None] == jnp.arange(experts, dtype=jnp.int32)[None, None, :]
    combine = jnp.sum(jnp.where(named, route_share[:, :, None], 0.0), axis=1)
    extra = -(-2 * experts // 128) * 128
    combine = jnp.pad(jnp.tile(combine, (1, 2)), ((0, 0), (0, extra - 2 * experts)))

    own_start = sect_pos * rows
    window = (back + 1) * rows
    padded = jnp.pad(segments, (back * rows, 0), constant_values=-1)
    key_seg = lax.dynamic_slice_in_dim(padded, own_start, window, 0)
    query_seg = key_seg[back * rows :]
    key_pos = jnp.arange(window, dtype=jnp.int32)
    query_pos = back * rows + jnp.arange(rows, dtype=jnp.int32)
    allowed = jnp.logical_and(
        key_seg[None, :] == query_seg[:, None], key_pos[None, :] <= query_pos[:, None]
    )
    bias = jnp.where(allowed, 0.0, negative_large).astype(jnp.float32)
    low_bits = []
    bit = 1
    while bit < top_bit:
        low_bits.append(bit)
        bit *= 2
    held = []
    first_hop = []
    for kv_index in range(kv_heads):
        attended = attend(queries, kv_blocks, bias, kv_index, kv_heads)
        held.append({0: attended})
        for bit in low_bits if kv_index % 2 else low_bits[::-1]:
            for offset in list(held[-1]):
                held[-1][offset ^ bit] = swap(held[-1][offset], "sect", bit)
            if len(held[-1]) == 2:
                first_hop.append(held[-1][bit])
    gathered = [[one[off] for off in range(top_bit)] for one in held]
    late = pieces // 2
    fetched[0][late:] = after(fetched[0][late:], first_hop)
    for piece in range(pieces):
        for other in range(1, group_count):
            fetched[other][piece] = swap(fetched[0][piece], "groups", other)

    if proj_weight.shape[1] % 128:
        stacked = jnp.stack([jnp.concatenate(fetched[g], axis=0) for g in range(group_count)])
        far = stacked[group_pos ^ jnp.arange(group_count)].reshape(proj_weight.shape)
        rows_all = jnp.concatenate([jnp.concatenate(held, axis=0) for held in gathered], axis=1)
        block = jnp.concatenate(
            [
                jnp.dot(rows_all, proj_weight, preferred_element_type=jnp.float32),
                jnp.dot(rows_all, far, preferred_element_type=jnp.float32),
            ],
            axis=1,
        ).reshape(top_bit, head_count, moe_rows, -1)
        kept = lax.dynamic_index_in_dim(block, head_pos, 1, keepdims=False)
        sent = lax.dynamic_index_in_dim(block, 1 - head_pos, 1, keepdims=False)
        sent = sent.astype(jnp.bfloat16)
    else:
        place = jnp.stack(
            [head_pos]
            + [(group_pos ^ g) * pieces + i for g in range(group_count) for i in range(pieces)]
        ).astype(jnp.int32)
        far_pieces = [fetched[g][i] for g in range(group_count) for i in range(pieces)]
        kept, sent = project(gathered, proj_weight, far_pieces, place)
    summed = (kept + swap(sent, "head", 1).astype(jnp.float32)).astype(jnp.bfloat16)
    own_parts = [summed[0]] + [swap(summed[off], "sect", off) for off in range(1, top_bit)]
    block_index = sect_pos ^ jnp.arange(sect_count, dtype=jnp.int32)
    hidden_mid, normed = norm_rows(
        jnp.stack(own_parts), residual, norm_gain, combine, experts, block_index
    )

    even = list(range(0, sect_count, 2))
    pieces_in = {0: normed}
    bit = top_bit
    while bit > 1:
        for off in list(pieces_in):
            pieces_in[off ^ bit] = swap(pieces_in[off], "sect", bit)
        bit //= 2

    own_expert = (sect_pos * head_count + head_pos).reshape(1).astype(jnp.int32)
    results, sums, sections = [], [], []
    for turn, off in enumerate(even):
        if turn > 1:
            (pieces_in[off],) = after([pieces_in[off]], results[turn - 2])
        pieces_in[off ^ 1] = swap(pieces_in[off], "sect", 1)
        chunk = []
        for o in (off, off ^ 1):
            chunk += [pieces_in[o], swap(pieces_in[o], "head", 1)]
        if turn > 1:
            done = sums[turn - 2 : turn - 1] + sections[max(0, turn - 3) : turn - 2]
            chunk = list(after(chunk, done))
        results.append(
            expert_rows(chunk, gate_weight, up_weight, down_weight, experts, own_expert)
        )
        kept, sent = results[-1]
        kept = kept + swap(sent, "head", 1).astype(jnp.float32)
        sums.append(kept[1].astype(jnp.bfloat16))
        section = kept[0] + swap(sums[-1], "sect", 1).astype(jnp.float32)
        sections.append(section.astype(jnp.bfloat16) if off else section)
    final = sections[0]
    for off, section in zip(even[1:], sections[1:]):
        final = final + swap(section, "sect", off).astype(jnp.float32)
    return (hidden_mid, final.astype(jnp.bfloat16))


def solution(mesh):
    placed = (
        P(("groups", "sect"), "head"),
        P(("groups", "sect"), "head"),
        P(("groups", "sect"), "head"),
        P("groups"),
        P("head", "sect"),
        P(("groups", "sect", "head"), None),
        P(),
        P(("groups", "sect", "head"), None),
        P(("groups", "sect", "head"), None),
        P(("sect", "head"), None, None),
        P(("sect", "head"), None, None),
        P(("sect", "head"), None, None),
    )
    return jax.shard_map(
        shards,
        mesh=mesh,
        in_specs=placed,
        out_specs=(P(("groups", "sect", "head"), None), P(("groups", "sect", "head"), None)),
        check_vma=False,
    )
```

```python
import functools
import math

import jax
import jax.numpy as jnp
from jax import lax
from jax.experimental import pallas as pl
from jax.experimental.pallas import tpu as pltpu
from jax.sharding import PartitionSpec as P

HEAD_WIDTH = 128

GRANT = 56 * 1024 * 1024

negative_large = -1e30
norm_eps = 1e-06


def swap(value, axis, bit):
    count = lax.axis_size(axis)
    return lax.ppermute(value, axis, [(i, i ^ bit) for i in range(count)])


def after(values, others):
    return lax.optimization_barrier((tuple(values), tuple(others)))[0]


def shift(value, axis, step):
    count = lax.axis_size(axis)
    return lax.ppermute(value, axis, [(i, i + step) for i in range(count - step)])


def attend_kernel(heads, scale, bias_ref, query_ref, *refs):
    *kv_refs, out_ref = refs
    rows = kv_refs[0].shape[0] // 2
    keys = jnp.concatenate([kv[:rows, :] for kv in kv_refs], axis=0)
    vals = jnp.concatenate([kv[rows:, :] for kv in kv_refs], axis=0)
    vals = jnp.concatenate([vals, jnp.ones_like(vals)], axis=1)
    for head in range(heads):
        cols = slice(head * HEAD_WIDTH, (head + 1) * HEAD_WIDTH)
        scores = lax.dot_general(
            query_ref[:, cols], keys, (((1,), (1,)), ((), ())), preferred_element_type=jnp.float32
        )
        scores = scores * scale + bias_ref[...]
        top = jnp.max(scores, axis=1, keepdims=True)
        weights = jnp.exp2(scores - top).astype(jnp.bfloat16)
        mixed = jnp.dot(weights, vals, preferred_element_type=jnp.float32)
        out_ref[:, cols] = (mixed[:, :HEAD_WIDTH] / mixed[:, HEAD_WIDTH:]).astype(jnp.bfloat16)


def attend(queries, kv_blocks, bias, kv_index, kv_heads):
    rows = queries.shape[0]
    width = queries.shape[1] // kv_heads
    heads = width // HEAD_WIDTH
    step_heads = min(4, heads)
    steps = heads // step_heads
    block = step_heads * HEAD_WIDTH
    keys = bias.shape[1]
    scale = math.log2(math.e) / math.sqrt(HEAD_WIDTH)
    return pl.pallas_call(
        functools.partial(attend_kernel, step_heads, scale),
        out_shape=jax.ShapeDtypeStruct((rows, width), jnp.bfloat16),
        grid=(steps,),
        in_specs=[
            pl.BlockSpec((rows, keys), lambda i: (0, 0)),
            pl.BlockSpec((rows, block), lambda i: (0, kv_index * steps + i)),
        ]
        + [pl.BlockSpec((2 * rows, HEAD_WIDTH), lambda i: (0, kv_index)) for _ in kv_blocks],
        out_specs=pl.BlockSpec((rows, block), lambda i: (0, i)),
        compiler_params=pltpu.CompilerParams(vmem_limit_bytes=GRANT),
        cost_estimate=pl.CostEstimate(
            flops=6 * rows * keys * width,
            bytes_accessed=4 * rows * width + 4 * rows * keys * len(kv_blocks),
            transcendentals=rows * keys * heads,
        ),
        name="attend",
    )(bias, queries, *kv_blocks)


def norm_kernel(experts, blocks_ref, residual_ref, gain_ref, combine_ref, *refs):
    *part_refs, hidden_ref, normed_ref = refs
    offsets = len(part_refs)
    rows, width = part_refs[0].shape
    half = width // 2
    columns = 2 * offsets * half
    total = jnp.zeros((rows, 1), jnp.float32)
    for off in range(offsets):
        for upper in range(2):
            col = pl.multiple_of(blocks_ref[off + upper * offsets] * half, half)
            cols = pl.ds(col, half)
            part = part_refs[off][:, upper * half : (upper + 1) * half]
            hidden = (residual_ref[:, cols].astype(jnp.float32) + part).astype(jnp.bfloat16)
            hidden_ref[:, cols] = hidden
            wide = hidden.astype(jnp.float32)
            total = total + jnp.sum(wide * wide, axis=1, keepdims=True)
    inverse = lax.rsqrt(total / columns + norm_eps)
    wide = hidden_ref[...].astype(jnp.float32)
    wide = wide * inverse * gain_ref[...].astype(jnp.float32)
    normed_ref[:, :columns] = wide.astype(jnp.bfloat16)
    normed_ref[:, columns:] = split_combine(combine_ref[...], experts)


def split_combine(combine, experts):
    high = combine.astype(jnp.bfloat16).astype(jnp.float32)
    lane = lax.broadcasted_iota(jnp.int32, combine.shape, 1)
    return jnp.where(lane < experts, high, combine - high).astype(jnp.bfloat16)


def norm_rows(parts, residual, gain, combine, experts, block_index):
    offsets = len(parts)
    rows, width = parts[0].shape
    if (width // 2) % 128:
        blocks = jnp.stack(parts).reshape(offsets, rows, 2, width // 2).transpose(2, 0, 1, 3)
        blocks = blocks.reshape(2 * offsets, rows, width // 2)[block_index]
        wide = blocks.transpose(1, 0, 2).reshape(residual.shape).astype(jnp.float32)
        hidden = (residual.astype(jnp.float32) + wide).astype(jnp.bfloat16)
        wide = hidden.astype(jnp.float32)
        inverse = lax.rsqrt(jnp.mean(wide * wide, axis=1, keepdims=True) + norm_eps)
        normed = (wide * inverse * gain.astype(jnp.float32)[None, :]).astype(jnp.bfloat16)
        high = lax.reduce_precision(combine, 8, 7)
        lane = lax.broadcasted_iota(jnp.int32, combine.shape, 1)
        split = jnp.where(lane < experts, high, combine - high).astype(jnp.bfloat16)
        return hidden, jnp.concatenate([normed, split], axis=1)
    vmem = pl.BlockSpec(memory_space=pltpu.VMEM)
    return pl.pallas_call(
        functools.partial(norm_kernel, experts),
        out_shape=(
            jax.ShapeDtypeStruct(residual.shape, jnp.bfloat16),
            jax.ShapeDtypeStruct((rows, residual.shape[1] + combine.shape[1]), jnp.bfloat16),
        ),
        in_specs=[pl.BlockSpec(memory_space=pltpu.SMEM)] + [vmem] * (3 + offsets),
        out_specs=(vmem, vmem),
        name="norm_rows",
    )(block_index, residual, gain.reshape(1, -1), combine, *parts)


def project_kernel(offset_lists, rows, place_ref, *refs):
    kv_heads, offsets = len(offset_lists), len(offset_lists[0])
    count = kv_heads * offsets
    rows_refs = refs[: 2 * kv_heads]
    own_ref = refs[2 * kv_heads]
    *far_refs, kept_ref, sent_ref, all_ref, near_ref, upper_ref, sems = refs[2 * kv_heads + 1 :]
    head = place_ref[0]
    width = rows_refs[0].shape[1]
    half = rows // 2
    depth = far_refs[0].shape[0]
    copies = [pltpu.make_async_copy(own_ref, near_ref, sems.at[count])]
    for kv_index in range(kv_heads):
        for position, off in enumerate(offset_lists[kv_index]):
            source = rows_refs[2 * kv_index + 2 * position // offsets]
            start = position % (offsets // 2) * rows
            target = all_ref.at[pl.ds(off * rows, rows), pl.ds(kv_index * width, width)]
            copies.append(
                pltpu.make_async_copy(
                    source.at[pl.ds(start, rows), :], target, sems.at[kv_index * offsets + position]
                )
            )
    far_copies = []
    for index, far_ref in enumerate(far_refs):
        target = upper_ref.at[pl.ds(index * depth, depth), :]
        far_copies.append(pltpu.make_async_copy(far_ref, target, sems.at[count + 1 + index]))
    for copy in copies + far_copies:
        copy.start()
    for copy in copies:
        copy.wait()
    near = jnp.dot(all_ref[...], near_ref[...], preferred_element_type=jnp.float32)
    far = None
    for index, copy in enumerate(far_copies):
        copy.wait()
        start = pl.multiple_of(place_ref[1 + index] * depth, depth)
        product = jnp.dot(
            all_ref[:, pl.ds(start, depth)],
            upper_ref[index * depth : (index + 1) * depth, :],
            preferred_element_type=jnp.float32,
        )
        far = product if far is None else far + product
    columns = near.shape[1]
    for off in range(offsets):
        for upper, block in enumerate((near, far)):
            cols = slice(upper * columns, (upper + 1) * columns)
            first = block[off * rows : off * rows + half]
            second = block[off * rows + half : (off + 1) * rows]
            kept_ref[off, :, cols] = jnp.where(head == 0, first, second)
            sent_ref[off, :, cols] = jnp.where(head == 0, second, first).astype(jnp.bfloat16)


def project(pieces, own_weight, far_pieces, place):
    kv_heads, offsets = len(pieces), len(pieces[0][1])
    flat = [part for parts, _ in pieces for part in parts]
    rows, width = 2 * flat[0].shape[0] // offsets, flat[0].shape[1]
    columns = own_weight.shape[1]
    vmem = pl.BlockSpec(memory_space=pltpu.VMEM)
    offset_lists = [offset_list for _, offset_list in pieces]
    shape = (offsets, rows // 2, 2 * columns)
    return pl.pallas_call(
        functools.partial(project_kernel, offset_lists, rows),
        out_shape=(
            jax.ShapeDtypeStruct(shape, jnp.float32),
            jax.ShapeDtypeStruct(shape, jnp.bfloat16),
        ),
        in_specs=[pl.BlockSpec(memory_space=pltpu.SMEM)]
        + [pl.BlockSpec(memory_space=pl.ANY)] * (len(flat) + 1 + len(far_pieces)),
        out_specs=(vmem, vmem),
        scratch_shapes=[
            pltpu.VMEM((offsets * rows, kv_heads * width), jnp.bfloat16),
            pltpu.VMEM(own_weight.shape, jnp.bfloat16),
            pltpu.VMEM(own_weight.shape, jnp.bfloat16),
            pltpu.SemaphoreType.DMA((kv_heads * offsets + 1 + len(far_pieces),)),
        ],
        compiler_params=pltpu.CompilerParams(vmem_limit_bytes=GRANT),
        cost_estimate=pl.CostEstimate(
            flops=4 * offsets * rows * kv_heads * width * columns,
            bytes_accessed=4 * kv_heads * width * columns,
            transcendentals=0,
        ),
        name="project",
    )(place, *flat, own_weight, *far_pieces)


def expert_kernel(experts, pieces, place_ref, *refs):
    piece_refs = refs[:pieces]
    gate_ref, up_ref, down_ref, kept_ref, sent_ref = refs[pieces : pieces + 5]
    rows_ref, mid_ref, sems = refs[pieces + 5 :]
    rows = piece_refs[0].shape[0]
    depth, inner = gate_ref.shape[1:]
    copies = [
        pltpu.make_async_copy(ref, rows_ref.at[pl.ds(i * rows, rows), :], sems.at[i])
        for i, ref in enumerate(piece_refs)
    ]
    for copy in copies:
        copy.start()
    for copy in copies:
        copy.wait()
    extra = rows_ref[:, depth:].astype(jnp.float32)
    lane = lax.broadcasted_iota(jnp.int32, extra.shape, 1)
    own = jnp.logical_or(lane == place_ref[0], lane == place_ref[0] + experts)
    share = jnp.sum(jnp.where(own, extra, 0.0), axis=1, keepdims=True)
    tile = math.gcd(inner, 256)
    for start in range(0, inner, tile):
        cols = slice(start, start + tile)
        flat = rows_ref[:, :depth]
        gate = jnp.dot(flat, gate_ref[0, :, cols], preferred_element_type=jnp.float32)
        up = jnp.dot(flat, up_ref[0, :, cols], preferred_element_type=jnp.float32)
        mid_ref[:, cols] = (gate / (1.0 + jnp.exp(-gate)) * up).astype(jnp.bfloat16)
    tile = math.gcd(depth, 512)
    for start in range(0, depth, tile):
        cols = slice(start, start + tile)
        out = jnp.dot(mid_ref[...], down_ref[0, :, cols], preferred_element_type=jnp.float32)
        out = out.astype(jnp.bfloat16).astype(jnp.float32) * share
        for index in range(pieces):
            part = out[index * rows : (index + 1) * rows]
            if index % 2:
                sent_ref[index // 2, :, cols] = part.astype(jnp.bfloat16)
            else:
                kept_ref[index // 2, :, cols] = part


def stream_kernel(experts, pieces, place_ref, *refs):
    piece_refs = refs[:pieces]
    gate_hbm, up_hbm, down_hbm, kept_ref, sent_ref = refs[pieces : pieces + 5]
    rows_ref, mid_ref, gate_ref, up_ref, down_ref, sems = refs[pieces + 5 :]
    rows = piece_refs[0].shape[0]
    depth, inner = gate_ref.shape
    inner_tile, depth_tile = math.gcd(inner, 256), math.gcd(depth, 512)
    inner_tiles, depth_tiles = inner // inner_tile, depth // depth_tile

    def tile(source, target, start, size, sem):
        cols = pl.ds(start, size)
        return pltpu.make_async_copy(source.at[0, :, cols], target.at[:, cols], sems.at[sem])

    row_copies = [
        pltpu.make_async_copy(ref, rows_ref.at[pl.ds(i * rows, rows), :], sems.at[i])
        for i, ref in enumerate(piece_refs)
    ]
    base = pieces
    first_copies = [
        (
            tile(gate_hbm, gate_ref, i * inner_tile, inner_tile, base + 2 * i),
            tile(up_hbm, up_ref, i * inner_tile, inner_tile, base + 2 * i + 1),
        )
        for i in range(inner_tiles)
    ]
    base += 2 * inner_tiles
    second_copies = [
        tile(down_hbm, down_ref, i * depth_tile, depth_tile, base + i) for i in range(depth_tiles)
    ]
    for copy in row_copies + [c for pair in first_copies for c in pair] + second_copies:
        copy.start()
    for copy in row_copies:
        copy.wait()
    extra = rows_ref[:, depth:].astype(jnp.float32)
    lane = lax.broadcasted_iota(jnp.int32, extra.shape, 1)
    own = jnp.logical_or(lane == place_ref[0], lane == place_ref[0] + experts)
    share = jnp.sum(jnp.where(own, extra, 0.0), axis=1, keepdims=True)
    for i in range(inner_tiles):
        cols = slice(i * inner_tile, (i + 1) * inner_tile)
        for copy in first_copies[i]:
            copy.wait()
        flat = rows_ref[:, :depth]
        gate = jnp.dot(flat, gate_ref[:, cols], preferred_element_type=jnp.float32)
        up = jnp.dot(flat, up_ref[:, cols], preferred_element_type=jnp.float32)
        mid_ref[:, cols] = (gate / (1.0 + jnp.exp(-gate)) * up).astype(jnp.bfloat16)
    for i in range(depth_tiles):
        cols = slice(i * depth_tile, (i + 1) * depth_tile)
        second_copies[i].wait()
        out = jnp.dot(mid_ref[...], down_ref[:, cols], preferred_element_type=jnp.float32)
        out = out.astype(jnp.bfloat16).astype(jnp.float32) * share
        for index in range(pieces):
            part = out[index * rows : (index + 1) * rows]
            if index % 2:
                sent_ref[index // 2, :, cols] = part.astype(jnp.bfloat16)
            else:
                kept_ref[index // 2, :, cols] = part


def expert_rows(pieces, gate_weight, up_weight, down_weight, experts, place, stream):
    rows = pieces[0].shape[0]
    depth, inner = gate_weight.shape[1:]
    count = len(pieces)
    vmem = pl.BlockSpec(memory_space=pltpu.VMEM)
    shape = (count // 2, rows, depth)
    held, copies = [], count
    if stream:
        held = [pltpu.VMEM(w.shape[1:], jnp.bfloat16) for w in (gate_weight, up_weight, down_weight)]
        copies += 2 * (inner // math.gcd(inner, 256)) + depth // math.gcd(depth, 512)
    return pl.pallas_call(
        functools.partial(stream_kernel if stream else expert_kernel, experts, count),
        out_shape=(
            jax.ShapeDtypeStruct(shape, jnp.float32),
            jax.ShapeDtypeStruct(shape, jnp.bfloat16),
        ),
        in_specs=[pl.BlockSpec(memory_space=pltpu.SMEM)]
        + [pl.BlockSpec(memory_space=pl.ANY)] * count
        + [pl.BlockSpec(memory_space=pl.ANY) if stream else vmem] * 3,
        out_specs=(vmem, vmem),
        scratch_shapes=[
            pltpu.VMEM((count * rows, pieces[0].shape[1]), jnp.bfloat16),
            pltpu.VMEM((count * rows, inner), jnp.bfloat16),
        ]
        + held
        + [pltpu.SemaphoreType.DMA((copies,))],
        compiler_params=pltpu.CompilerParams(vmem_limit_bytes=GRANT if stream else 16 * 1024 * 1024),
        cost_estimate=pl.CostEstimate(
            flops=6 * count * rows * depth * inner,
            bytes_accessed=6 * depth * inner,
            transcendentals=count * rows * inner,
        ),
        name="expert_rows",
    )(place, *pieces, gate_weight, up_weight, down_weight)


def shards(
    queries,
    packed_key_rows,
    values,
    segments,
    proj_weight,
    residual,
    norm_gain,
    expert_ids,
    route_weights,
    gate_weight,
    up_weight,
    down_weight,
):
    rows = queries.shape[0]
    total_rows = segments.shape[0]
    sect_count = lax.axis_size("sect")
    head_count = lax.axis_size("head")
    group_count = lax.axis_size("groups")
    sect_pos = lax.axis_index("sect")
    head_pos = lax.axis_index("head")
    group_pos = lax.axis_index("groups")
    kv_heads = packed_key_rows.shape[1] // HEAD_WIDTH
    experts = sect_count * head_count
    moe_rows = residual.shape[0]
    top_bit = sect_count // 2

    back = min(sect_count - 1, -(-(total_rows // 2 - 1) // rows))
    own_kv = jnp.concatenate([packed_key_rows, values], axis=0)
    kv_blocks = [shift(own_kv, "sect", step) for step in range(back, 0, -1)] + [own_kv]

    depth = proj_weight.shape[0]
    part_depth = depth // group_count
    pieces = 2
    piece_depth = part_depth // pieces
    source, *kv_blocks = lax.optimization_barrier((proj_weight, *kv_blocks))
    fetched = [[None] * pieces for _ in range(group_count)]
    for piece in range(pieces):
        start = group_pos * part_depth + piece * piece_depth
        mine = lax.dynamic_slice_in_dim(source, start, piece_depth, 0)
        fetched[0][piece] = swap(mine, "sect", top_bit)
    route_share = route_weights / jnp.sum(route_weights, axis=1, keepdims=True)
    named = expert_ids[:, :, None] == jnp.arange(experts, dtype=jnp.int32)[None, None, :]
    combine = jnp.sum(jnp.where(named, route_share[:, :, None], 0.0), axis=1)
    extra = -(-2 * experts // 128) * 128
    combine = jnp.pad(jnp.tile(combine, (1, 2)), ((0, 0), (0, extra - 2 * experts)))

    own_start = sect_pos * rows
    window = (back + 1) * rows
    padded = jnp.pad(segments, (back * rows, 0), constant_values=-1)
    key_seg = lax.dynamic_slice_in_dim(padded, own_start, window, 0)
    query_seg = key_seg[back * rows :]
    key_pos = jnp.arange(window, dtype=jnp.int32)
    query_pos = back * rows + jnp.arange(rows, dtype=jnp.int32)
    allowed = jnp.logical_and(
        key_seg[None, :] == query_seg[:, None], key_pos[None, :] <= query_pos[:, None]
    )
    bias = jnp.where(allowed, 0.0, negative_large).astype(jnp.float32)
    low_bits = []
    bit = 1
    while bit < top_bit:
        low_bits.append(bit)
        bit *= 2
    gathered = []
    first_hop = []
    for kv_index in range(kv_heads):
        parts, offsets = [attend(queries, kv_blocks, bias, kv_index, kv_heads)], [0]
        for bit in low_bits if kv_index % 2 else low_bits[::-1]:
            both = jnp.concatenate(parts, axis=0) if len(parts) > 1 else parts[0]
            parts = [both, swap(both, "sect", bit)]
            offsets += [off ^ bit for off in offsets]
            if len(offsets) == 2:
                first_hop.append(parts[1])
        gathered.append((parts, offsets))
    late = pieces // 2
    fetched[0][late:] = after(fetched[0][late:], first_hop)
    for piece in range(pieces):
        for other in range(1, group_count):
            fetched[other][piece] = swap(fetched[0][piece], "groups", other)

    if proj_weight.shape[1] % 128:
        stacked = jnp.stack([jnp.concatenate(fetched[g], axis=0) for g in range(group_count)])
        far = stacked[group_pos ^ jnp.arange(group_count)].reshape(proj_weight.shape)
        ordered = []
        for parts, offsets in gathered:
            every = jnp.concatenate(parts, axis=0).reshape(top_bit, rows, -1)
            order = [offsets.index(off) for off in range(top_bit)]
            ordered.append(every[jnp.array(order)].reshape(top_bit * rows, -1))
        rows_all = jnp.concatenate(ordered, axis=1)
        block = jnp.concatenate(
            [
                jnp.dot(rows_all, proj_weight, preferred_element_type=jnp.float32),
                jnp.dot(rows_all, far, preferred_element_type=jnp.float32),
            ],
            axis=1,
        ).reshape(top_bit, head_count, moe_rows, -1)
        kept = lax.dynamic_index_in_dim(block, head_pos, 1, keepdims=False)
        sent = lax.dynamic_index_in_dim(block, 1 - head_pos, 1, keepdims=False)
        sent = sent.astype(jnp.bfloat16)
    else:
        place = jnp.stack(
            [head_pos]
            + [(group_pos ^ g) * pieces + i for g in range(group_count) for i in range(pieces)]
        ).astype(jnp.int32)
        far_pieces = [fetched[g][i] for g in range(group_count) for i in range(pieces)]
        kept, sent = project(gathered, proj_weight, far_pieces, place)
    summed = (kept + swap(sent, "head", 1).astype(jnp.float32)).astype(jnp.bfloat16)
    own_parts = [summed[0]] + [swap(summed[off], "sect", off) for off in range(1, top_bit)]
    block_index = sect_pos ^ jnp.arange(sect_count, dtype=jnp.int32)
    hidden_mid, normed = norm_rows(
        own_parts, residual, norm_gain, combine, experts, block_index
    )

    even = list(range(0, sect_count, 2))
    pieces_in = {0: normed}
    bit = top_bit
    while bit > 1:
        for off in list(pieces_in):
            pieces_in[off ^ bit] = swap(pieces_in[off], "sect", bit)
        bit //= 2

    own_expert = (sect_pos * head_count + head_pos).reshape(1).astype(jnp.int32)
    results, sums, keeps, sections = [], [], [], []
    for turn, off in enumerate(even):
        pieces_in[off ^ 1] = swap(pieces_in[off], "sect", 1)
        chunk = []
        for o in (off, off ^ 1):
            chunk += [pieces_in[o], swap(pieces_in[o], "head", 1)]
        results.append(
            expert_rows(
                chunk, gate_weight, up_weight, down_weight, experts, own_expert, turn == 0
            )
        )
        kept, sent = results[-1]
        kept = kept + swap(sent, "head", 1).astype(jnp.float32)
        keeps.append(kept[0])
        sums.append(kept[1].astype(jnp.bfloat16))
    lead = [sums[i] for i, off in enumerate(even) if off >= top_bit]
    for turn, off in enumerate(even):
        outgoing = sums[turn]
        if off < top_bit:
            (outgoing,) = after([outgoing], lead)
        section = keeps[turn] + swap(outgoing, "sect", 1).astype(jnp.float32)
        sections.append(section.astype(jnp.bfloat16) if off else section)
    final = sections[0]
    for off, section in zip(even[1:], sections[1:]):
        final = final + swap(section, "sect", off).astype(jnp.float32)
    return (hidden_mid, final.astype(jnp.bfloat16))


def solution(mesh):
    placed = (
        P(("groups", "sect"), "head"),
        P(("groups", "sect"), "head"),
        P(("groups", "sect"), "head"),
        P("groups"),
        P("head", "sect"),
        P(("groups", "sect", "head"), None),
        P(),
        P(("groups", "sect", "head"), None),
        P(("groups", "sect", "head"), None),
        P(("sect", "head"), None, None),
        P(("sect", "head"), None, None),
        P(("sect", "head"), None, None),
    )
    return jax.shard_map(
        shards,
        mesh=mesh,
        in_specs=placed,
        out_specs=(P(("groups", "sect", "head"), None), P(("groups", "sect", "head"), None)),
        check_vma=False,
    )
```

```python
import functools
import math

import jax
import jax.numpy as jnp
from jax import lax
from jax.experimental import pallas as pl
from jax.experimental.pallas import tpu as pltpu
from jax.sharding import PartitionSpec as P

HEAD_WIDTH = 128

GRANT = 56 * 1024 * 1024

negative_large = -1e30
norm_eps = 1e-06


def swap(value, axis, bit):
    count = lax.axis_size(axis)
    return lax.ppermute(value, axis, [(i, i ^ bit) for i in range(count)])


def after(values, others):
    return lax.optimization_barrier((tuple(values), tuple(others)))[0]


def shift(value, axis, step):
    count = lax.axis_size(axis)
    return lax.ppermute(value, axis, [(i, i + step) for i in range(count - step)])


def attend_kernel(heads, scale, bias_ref, query_ref, *refs):
    *kv_refs, out_ref = refs
    rows = kv_refs[0].shape[0] // 2
    keys = jnp.concatenate([kv[:rows, :] for kv in kv_refs], axis=0)
    vals = jnp.concatenate([kv[rows:, :] for kv in kv_refs], axis=0)
    vals = jnp.concatenate([vals, jnp.ones_like(vals)], axis=1)
    for head in range(heads):
        cols = slice(head * HEAD_WIDTH, (head + 1) * HEAD_WIDTH)
        scores = lax.dot_general(
            query_ref[:, cols], keys, (((1,), (1,)), ((), ())), preferred_element_type=jnp.float32
        )
        scores = scores * scale + bias_ref[...]
        top = jnp.max(scores, axis=1, keepdims=True)
        weights = jnp.exp2(scores - top).astype(jnp.bfloat16)
        mixed = jnp.dot(weights, vals, preferred_element_type=jnp.float32)
        out_ref[:, cols] = (mixed[:, :HEAD_WIDTH] / mixed[:, HEAD_WIDTH:]).astype(jnp.bfloat16)


def attend(queries, kv_blocks, bias, kv_index, kv_heads):
    rows = queries.shape[0]
    width = queries.shape[1] // kv_heads
    heads = width // HEAD_WIDTH
    step_heads = min(4, heads)
    steps = heads // step_heads
    block = step_heads * HEAD_WIDTH
    keys = bias.shape[1]
    scale = math.log2(math.e) / math.sqrt(HEAD_WIDTH)
    return pl.pallas_call(
        functools.partial(attend_kernel, step_heads, scale),
        out_shape=jax.ShapeDtypeStruct((rows, width), jnp.bfloat16),
        grid=(steps,),
        in_specs=[
            pl.BlockSpec((rows, keys), lambda i: (0, 0)),
            pl.BlockSpec((rows, block), lambda i: (0, kv_index * steps + i)),
        ]
        + [pl.BlockSpec((2 * rows, HEAD_WIDTH), lambda i: (0, kv_index)) for _ in kv_blocks],
        out_specs=pl.BlockSpec((rows, block), lambda i: (0, i)),
        compiler_params=pltpu.CompilerParams(vmem_limit_bytes=GRANT),
        cost_estimate=pl.CostEstimate(flops=1, bytes_accessed=1, transcendentals=0),
        name="attend",
    )(bias, queries, *kv_blocks)


def norm_kernel(experts, blocks_ref, residual_ref, gain_ref, combine_ref, *refs):
    *part_refs, hidden_ref, normed_ref = refs
    offsets = len(part_refs)
    rows, width = part_refs[0].shape
    half = width // 2
    columns = 2 * offsets * half
    total = jnp.zeros((rows, 1), jnp.float32)
    for off in range(offsets):
        for upper in range(2):
            col = pl.multiple_of(blocks_ref[off + upper * offsets] * half, half)
            cols = pl.ds(col, half)
            part = part_refs[off][:, upper * half : (upper + 1) * half]
            hidden = (residual_ref[:, cols].astype(jnp.float32) + part).astype(jnp.bfloat16)
            hidden_ref[:, cols] = hidden
            wide = hidden.astype(jnp.float32)
            total = total + jnp.sum(wide * wide, axis=1, keepdims=True)
    inverse = lax.rsqrt(total / columns + norm_eps)
    wide = hidden_ref[...].astype(jnp.float32)
    wide = wide * inverse * gain_ref[...].astype(jnp.float32)
    normed_ref[:, :columns] = wide.astype(jnp.bfloat16)
    normed_ref[:, columns:] = split_combine(combine_ref[...], experts)


def split_combine(combine, experts):
    high = combine.astype(jnp.bfloat16).astype(jnp.float32)
    lane = lax.broadcasted_iota(jnp.int32, combine.shape, 1)
    return jnp.where(lane < experts, high, combine - high).astype(jnp.bfloat16)


def norm_rows(parts, residual, gain, combine, experts, block_index):
    offsets = len(parts)
    rows, width = parts[0].shape
    if (width // 2) % 128:
        blocks = jnp.stack(parts).reshape(offsets, rows, 2, width // 2).transpose(2, 0, 1, 3)
        blocks = blocks.reshape(2 * offsets, rows, width // 2)[block_index]
        wide = blocks.transpose(1, 0, 2).reshape(residual.shape).astype(jnp.float32)
        hidden = (residual.astype(jnp.float32) + wide).astype(jnp.bfloat16)
        wide = hidden.astype(jnp.float32)
        inverse = lax.rsqrt(jnp.mean(wide * wide, axis=1, keepdims=True) + norm_eps)
        normed = (wide * inverse * gain.astype(jnp.float32)[None, :]).astype(jnp.bfloat16)
        high = lax.reduce_precision(combine, 8, 7)
        lane = lax.broadcasted_iota(jnp.int32, combine.shape, 1)
        split = jnp.where(lane < experts, high, combine - high).astype(jnp.bfloat16)
        return hidden, jnp.concatenate([normed, split], axis=1)
    vmem = pl.BlockSpec(memory_space=pltpu.VMEM)
    return pl.pallas_call(
        functools.partial(norm_kernel, experts),
        out_shape=(
            jax.ShapeDtypeStruct(residual.shape, jnp.bfloat16),
            jax.ShapeDtypeStruct((rows, residual.shape[1] + combine.shape[1]), jnp.bfloat16),
        ),
        in_specs=[pl.BlockSpec(memory_space=pltpu.SMEM)] + [vmem] * (3 + offsets),
        out_specs=(vmem, vmem),
        name="norm_rows",
    )(block_index, residual, gain.reshape(1, -1), combine, *parts)


def project_kernel(offset_lists, rows, place_ref, *refs):
    kv_heads, offsets = len(offset_lists), len(offset_lists[0])
    count = kv_heads * offsets
    rows_refs = refs[: 2 * kv_heads]
    own_ref = refs[2 * kv_heads]
    *far_refs, kept_ref, sent_ref, all_ref, near_ref, upper_ref, sems = refs[2 * kv_heads + 1 :]
    head = place_ref[0]
    width = rows_refs[0].shape[1]
    half = rows // 2
    depth = far_refs[0].shape[0]
    copies = [pltpu.make_async_copy(own_ref, near_ref, sems.at[count])]
    for kv_index in range(kv_heads):
        for position, off in enumerate(offset_lists[kv_index]):
            source = rows_refs[2 * kv_index + 2 * position // offsets]
            start = position % (offsets // 2) * rows
            target = all_ref.at[pl.ds(off * rows, rows), pl.ds(kv_index * width, width)]
            copies.append(
                pltpu.make_async_copy(
                    source.at[pl.ds(start, rows), :], target, sems.at[kv_index * offsets + position]
                )
            )
    far_copies = []
    for index, far_ref in enumerate(far_refs):
        target = upper_ref.at[pl.ds(index * depth, depth), :]
        far_copies.append(pltpu.make_async_copy(far_ref, target, sems.at[count + 1 + index]))
    for copy in copies + far_copies:
        copy.start()
    for copy in copies:
        copy.wait()
    near = jnp.dot(all_ref[...], near_ref[...], preferred_element_type=jnp.float32)
    far = None
    for index, copy in enumerate(far_copies):
        copy.wait()
        start = pl.multiple_of(place_ref[1 + index] * depth, depth)
        product = jnp.dot(
            all_ref[:, pl.ds(start, depth)],
            upper_ref[index * depth : (index + 1) * depth, :],
            preferred_element_type=jnp.float32,
        )
        far = product if far is None else far + product
    columns = near.shape[1]
    for off in range(offsets):
        for upper, block in enumerate((near, far)):
            cols = slice(upper * columns, (upper + 1) * columns)
            first = block[off * rows : off * rows + half]
            second = block[off * rows + half : (off + 1) * rows]
            kept_ref[off, :, cols] = jnp.where(head == 0, first, second)
            sent_ref[off, :, cols] = jnp.where(head == 0, second, first).astype(jnp.bfloat16)


def project(pieces, own_weight, far_pieces, place):
    kv_heads, offsets = len(pieces), len(pieces[0][1])
    flat = [part for parts, _ in pieces for part in parts]
    rows, width = 2 * flat[0].shape[0] // offsets, flat[0].shape[1]
    columns = own_weight.shape[1]
    vmem = pl.BlockSpec(memory_space=pltpu.VMEM)
    offset_lists = [offset_list for _, offset_list in pieces]
    shape = (offsets, rows // 2, 2 * columns)
    return pl.pallas_call(
        functools.partial(project_kernel, offset_lists, rows),
        out_shape=(
            jax.ShapeDtypeStruct(shape, jnp.float32),
            jax.ShapeDtypeStruct(shape, jnp.bfloat16),
        ),
        in_specs=[pl.BlockSpec(memory_space=pltpu.SMEM)]
        + [pl.BlockSpec(memory_space=pl.ANY)] * (len(flat) + 1 + len(far_pieces)),
        out_specs=(vmem, vmem),
        scratch_shapes=[
            pltpu.VMEM((offsets * rows, kv_heads * width), jnp.bfloat16),
            pltpu.VMEM(own_weight.shape, jnp.bfloat16),
            pltpu.VMEM(own_weight.shape, jnp.bfloat16),
            pltpu.SemaphoreType.DMA((kv_heads * offsets + 1 + len(far_pieces),)),
        ],
        compiler_params=pltpu.CompilerParams(vmem_limit_bytes=GRANT),
        cost_estimate=pl.CostEstimate(flops=1, bytes_accessed=1, transcendentals=0),
        name="project",
    )(place, *flat, own_weight, *far_pieces)


def expert_kernel(experts, pieces, place_ref, *refs):
    piece_refs = refs[:pieces]
    gate_ref, up_ref, down_ref, kept_ref, sent_ref = refs[pieces : pieces + 5]
    rows_ref, mid_ref, sems = refs[pieces + 5 :]
    rows = piece_refs[0].shape[0]
    depth, inner = gate_ref.shape[1:]
    copies = [
        pltpu.make_async_copy(ref, rows_ref.at[pl.ds(i * rows, rows), :], sems.at[i])
        for i, ref in enumerate(piece_refs)
    ]
    for copy in copies:
        copy.start()
    for copy in copies:
        copy.wait()
    extra = rows_ref[:, depth:].astype(jnp.float32)
    lane = lax.broadcasted_iota(jnp.int32, extra.shape, 1)
    own = jnp.logical_or(lane == place_ref[0], lane == place_ref[0] + experts)
    share = jnp.sum(jnp.where(own, extra, 0.0), axis=1, keepdims=True)
    tile = math.gcd(inner, 256)
    for start in range(0, inner, tile):
        cols = slice(start, start + tile)
        flat = rows_ref[:, :depth]
        gate = jnp.dot(flat, gate_ref[0, :, cols], preferred_element_type=jnp.float32)
        up = jnp.dot(flat, up_ref[0, :, cols], preferred_element_type=jnp.float32)
        mid_ref[:, cols] = (gate / (1.0 + jnp.exp(-gate)) * up).astype(jnp.bfloat16)
    tile = math.gcd(depth, 512)
    for start in range(0, depth, tile):
        cols = slice(start, start + tile)
        out = jnp.dot(mid_ref[...], down_ref[0, :, cols], preferred_element_type=jnp.float32)
        out = out.astype(jnp.bfloat16).astype(jnp.float32) * share
        for index in range(pieces):
            part = out[index * rows : (index + 1) * rows]
            if index % 2:
                sent_ref[index // 2, :, cols] = part.astype(jnp.bfloat16)
            else:
                kept_ref[index // 2, :, cols] = part


def stream_kernel(experts, pieces, place_ref, *refs):
    piece_refs = refs[:pieces]
    gate_hbm, up_hbm, down_hbm, kept_ref, sent_ref = refs[pieces : pieces + 5]
    rows_ref, mid_ref, gate_ref, up_ref, down_ref, sems = refs[pieces + 5 :]
    rows = piece_refs[0].shape[0]
    depth, inner = gate_ref.shape
    inner_tile, depth_tile = math.gcd(inner, 256), math.gcd(depth, 512)
    inner_tiles, depth_tiles = inner // inner_tile, depth // depth_tile

    def tile(source, target, start, size, sem):
        cols = pl.ds(start, size)
        return pltpu.make_async_copy(source.at[0, :, cols], target.at[:, cols], sems.at[sem])

    row_copies = [
        pltpu.make_async_copy(ref, rows_ref.at[pl.ds(i * rows, rows), :], sems.at[i])
        for i, ref in enumerate(piece_refs)
    ]
    base = pieces
    first_copies = [
        (
            tile(gate_hbm, gate_ref, i * inner_tile, inner_tile, base + 2 * i),
            tile(up_hbm, up_ref, i * inner_tile, inner_tile, base + 2 * i + 1),
        )
        for i in range(inner_tiles)
    ]
    base += 2 * inner_tiles
    second_copies = [
        tile(down_hbm, down_ref, i * depth_tile, depth_tile, base + i) for i in range(depth_tiles)
    ]
    for copy in row_copies + [c for pair in first_copies for c in pair] + second_copies:
        copy.start()
    for copy in row_copies:
        copy.wait()
    extra = rows_ref[:, depth:].astype(jnp.float32)
    lane = lax.broadcasted_iota(jnp.int32, extra.shape, 1)
    own = jnp.logical_or(lane == place_ref[0], lane == place_ref[0] + experts)
    share = jnp.sum(jnp.where(own, extra, 0.0), axis=1, keepdims=True)
    for i in range(inner_tiles):
        cols = slice(i * inner_tile, (i + 1) * inner_tile)
        for copy in first_copies[i]:
            copy.wait()
        flat = rows_ref[:, :depth]
        gate = jnp.dot(flat, gate_ref[:, cols], preferred_element_type=jnp.float32)
        up = jnp.dot(flat, up_ref[:, cols], preferred_element_type=jnp.float32)
        mid_ref[:, cols] = (gate / (1.0 + jnp.exp(-gate)) * up).astype(jnp.bfloat16)
    for i in range(depth_tiles):
        cols = slice(i * depth_tile, (i + 1) * depth_tile)
        second_copies[i].wait()
        out = jnp.dot(mid_ref[...], down_ref[:, cols], preferred_element_type=jnp.float32)
        out = out.astype(jnp.bfloat16).astype(jnp.float32) * share
        for index in range(pieces):
            part = out[index * rows : (index + 1) * rows]
            if index % 2:
                sent_ref[index // 2, :, cols] = part.astype(jnp.bfloat16)
            else:
                kept_ref[index // 2, :, cols] = part


def expert_rows(pieces, gate_weight, up_weight, down_weight, experts, place, stream):
    rows = pieces[0].shape[0]
    depth, inner = gate_weight.shape[1:]
    count = len(pieces)
    vmem = pl.BlockSpec(memory_space=pltpu.VMEM)
    shape = (count // 2, rows, depth)
    held, copies = [], count
    if stream:
        held = [pltpu.VMEM(w.shape[1:], jnp.bfloat16) for w in (gate_weight, up_weight, down_weight)]
        copies += 2 * (inner // math.gcd(inner, 256)) + depth // math.gcd(depth, 512)
    return pl.pallas_call(
        functools.partial(stream_kernel if stream else expert_kernel, experts, count),
        out_shape=(
            jax.ShapeDtypeStruct(shape, jnp.float32),
            jax.ShapeDtypeStruct(shape, jnp.bfloat16),
        ),
        in_specs=[pl.BlockSpec(memory_space=pltpu.SMEM)]
        + [pl.BlockSpec(memory_space=pl.ANY)] * count
        + [pl.BlockSpec(memory_space=pl.ANY) if stream else vmem] * 3,
        out_specs=(vmem, vmem),
        scratch_shapes=[
            pltpu.VMEM((count * rows, pieces[0].shape[1]), jnp.bfloat16),
            pltpu.VMEM((count * rows, inner), jnp.bfloat16),
        ]
        + held
        + [pltpu.SemaphoreType.DMA((copies,))],
        compiler_params=pltpu.CompilerParams(vmem_limit_bytes=GRANT if stream else 16 * 1024 * 1024),
        cost_estimate=pl.CostEstimate(flops=1, bytes_accessed=1, transcendentals=0),
        name="expert_rows",
    )(place, *pieces, gate_weight, up_weight, down_weight)


def shards(
    queries,
    packed_key_rows,
    values,
    segments,
    proj_weight,
    residual,
    norm_gain,
    expert_ids,
    route_weights,
    gate_weight,
    up_weight,
    down_weight,
):
    rows = queries.shape[0]
    total_rows = segments.shape[0]
    sect_count = lax.axis_size("sect")
    head_count = lax.axis_size("head")
    group_count = lax.axis_size("groups")
    sect_pos = lax.axis_index("sect")
    head_pos = lax.axis_index("head")
    group_pos = lax.axis_index("groups")
    kv_heads = packed_key_rows.shape[1] // HEAD_WIDTH
    experts = sect_count * head_count
    moe_rows = residual.shape[0]
    top_bit = sect_count // 2

    back = min(sect_count - 1, -(-(total_rows // 2 - 1) // rows))
    own_kv = jnp.concatenate([packed_key_rows, values], axis=0)
    kv_blocks = [shift(own_kv, "sect", step) for step in range(back, 0, -1)] + [own_kv]

    depth = proj_weight.shape[0]
    part_depth = depth // group_count
    pieces = 2
    piece_depth = part_depth // pieces
    source, *kv_blocks = lax.optimization_barrier((proj_weight, *kv_blocks))
    fetched = [[None] * pieces for _ in range(group_count)]
    for piece in range(pieces):
        start = group_pos * part_depth + piece * piece_depth
        mine = lax.dynamic_slice_in_dim(source, start, piece_depth, 0)
        fetched[0][piece] = swap(mine, "sect", top_bit)
    route_share = route_weights / jnp.sum(route_weights, axis=1, keepdims=True)
    named = expert_ids[:, :, None] == jnp.arange(experts, dtype=jnp.int32)[None, None, :]
    combine = jnp.sum(jnp.where(named, route_share[:, :, None], 0.0), axis=1)
    extra = -(-2 * experts // 128) * 128
    combine = jnp.pad(jnp.tile(combine, (1, 2)), ((0, 0), (0, extra - 2 * experts)))

    own_start = sect_pos * rows
    window = (back + 1) * rows
    padded = jnp.pad(segments, (back * rows, 0), constant_values=-1)
    key_seg = lax.dynamic_slice_in_dim(padded, own_start, window, 0)
    query_seg = key_seg[back * rows :]
    key_pos = jnp.arange(window, dtype=jnp.int32)
    query_pos = back * rows + jnp.arange(rows, dtype=jnp.int32)
    allowed = jnp.logical_and(
        key_seg[None, :] == query_seg[:, None], key_pos[None, :] <= query_pos[:, None]
    )
    bias = jnp.where(allowed, 0.0, negative_large).astype(jnp.float32)
    low_bits = []
    bit = 1
    while bit < top_bit:
        low_bits.append(bit)
        bit *= 2
    gathered = []
    first_hop = []
    for kv_index in range(kv_heads):
        parts, offsets = [attend(queries, kv_blocks, bias, kv_index, kv_heads)], [0]
        for bit in low_bits if kv_index % 2 else low_bits[::-1]:
            both = jnp.concatenate(parts, axis=0) if len(parts) > 1 else parts[0]
            parts = [both, swap(both, "sect", bit)]
            offsets += [off ^ bit for off in offsets]
            if len(offsets) == 2:
                first_hop.append(parts[1])
        gathered.append((parts, offsets))
    late = pieces // 2
    fetched[0][late:] = after(fetched[0][late:], first_hop)
    for piece in range(pieces):
        for other in range(1, group_count):
            fetched[other][piece] = swap(fetched[0][piece], "groups", other)

    if proj_weight.shape[1] % 128:
        stacked = jnp.stack([jnp.concatenate(fetched[g], axis=0) for g in range(group_count)])
        far = stacked[group_pos ^ jnp.arange(group_count)].reshape(proj_weight.shape)
        ordered = []
        for parts, offsets in gathered:
            every = jnp.concatenate(parts, axis=0).reshape(top_bit, rows, -1)
            order = [offsets.index(off) for off in range(top_bit)]
            ordered.append(every[jnp.array(order)].reshape(top_bit * rows, -1))
        rows_all = jnp.concatenate(ordered, axis=1)
        block = jnp.concatenate(
            [
                jnp.dot(rows_all, proj_weight, preferred_element_type=jnp.float32),
                jnp.dot(rows_all, far, preferred_element_type=jnp.float32),
            ],
            axis=1,
        ).reshape(top_bit, head_count, moe_rows, -1)
        kept = lax.dynamic_index_in_dim(block, head_pos, 1, keepdims=False)
        sent = lax.dynamic_index_in_dim(block, 1 - head_pos, 1, keepdims=False)
        sent = sent.astype(jnp.bfloat16)
    else:
        place = jnp.stack(
            [head_pos]
            + [(group_pos ^ g) * pieces + i for g in range(group_count) for i in range(pieces)]
        ).astype(jnp.int32)
        far_pieces = [fetched[g][i] for g in range(group_count) for i in range(pieces)]
        kept, sent = project(gathered, proj_weight, far_pieces, place)
    summed = (kept + swap(sent, "head", 1).astype(jnp.float32)).astype(jnp.bfloat16)
    own_parts = [summed[0]] + [swap(summed[off], "sect", off) for off in range(1, top_bit)]
    block_index = sect_pos ^ jnp.arange(sect_count, dtype=jnp.int32)
    hidden_mid, normed = norm_rows(
        own_parts, residual, norm_gain, combine, experts, block_index
    )

    even = list(range(0, sect_count, 2))
    pieces_in = {0: normed}
    bit = top_bit
    while bit > 1:
        for off in list(pieces_in):
            pieces_in[off ^ bit] = swap(pieces_in[off], "sect", bit)
        bit //= 2

    own_expert = (sect_pos * head_count + head_pos).reshape(1).astype(jnp.int32)
    results, sums, keeps, sections = [], [], [], []
    for turn, off in enumerate(even):
        pieces_in[off ^ 1] = swap(pieces_in[off], "sect", 1)
        chunk = []
        for o in (off, off ^ 1):
            chunk += [pieces_in[o], swap(pieces_in[o], "head", 1)]
        results.append(
            expert_rows(
                chunk, gate_weight, up_weight, down_weight, experts, own_expert, turn == 0
            )
        )
        kept, sent = results[-1]
        kept = kept + swap(sent, "head", 1).astype(jnp.float32)
        keeps.append(kept[0])
        sums.append(kept[1].astype(jnp.bfloat16))
    lead = [sums[i] for i, off in enumerate(even) if off >= top_bit]
    for turn, off in enumerate(even):
        outgoing = sums[turn]
        if off < top_bit:
            (outgoing,) = after([outgoing], lead)
        section = keeps[turn] + swap(outgoing, "sect", 1).astype(jnp.float32)
        sections.append(section.astype(jnp.bfloat16) if off else section)
    final = sections[0]
    for off, section in zip(even[1:], sections[1:]):
        final = final + swap(section, "sect", off).astype(jnp.float32)
    return (hidden_mid, final.astype(jnp.bfloat16))


def solution(mesh):
    placed = (
        P(("groups", "sect"), "head"),
        P(("groups", "sect"), "head"),
        P(("groups", "sect"), "head"),
        P("groups"),
        P("head", "sect"),
        P(("groups", "sect", "head"), None),
        P(),
        P(("groups", "sect", "head"), None),
        P(("groups", "sect", "head"), None),
        P(("sect", "head"), None, None),
        P(("sect", "head"), None, None),
        P(("sect", "head"), None, None),
    )
    return jax.shard_map(
        shards,
        mesh=mesh,
        in_specs=placed,
        out_specs=(P(("groups", "sect", "head"), None), P(("groups", "sect", "head"), None)),
        check_vma=False,
    )
```
